256 devices in a mesh: rows: 64 (over z, y, core), cols: 4 (over x).
Axes of the slice: x: 4, y: 4, z: 8, core: 2. Of those that a mesh axis runs over, the one named last changes fastest.
Arguments:
- stiffness: bfloat16 [1024, 16, 192, 192], P('rows', 'cols'), may hold values from -0.4375 to 0.4375
- neighbors: int32 [1024, 16], P('rows', 'cols'), may hold values from 0 to 1023, as said below
- live_counts: int32 [1024], P('rows'), may hold values from 8 to 16, as said below
- prolong: bfloat16 [1024, 192, 192], P('rows', 'cols'), may hold values from -0.59765625 to 0.59765625
- prolong_aggs: int32 [1024, 32], replicated, may hold values from 0 to 1023, as said below
Outputs:
- coarse_rows: float32 [6144, 672], P('rows', 'cols')
The draws below stay inside these ranges and needn't reach their ends.
Inputs may be any that keep to these rules, and one draw needn't show every extreme that they name: `neighbors`: each slot's column lies within 16 blocks of its row block; on every index of rows some slot reaches the first block of the index below and some the last block of the index above, clipped to the slab. `live_counts`: the first row block of every index of rows has all 16 slots live. `prolong_aggs`: the 32 aggregates of a row block are distinct, include the row block itself, and lie in the blocks of its own index of rows and of the indices just below and above.
All inputs are finite; a program needn't handle non-finite values.
Results may differ from the reference program's by a relative error of at most 0.0029.
Values may be sent and summed in bfloat16 or wider, within the bound.
No kernel may reach another device: no remote copies, remote signals or barrier semaphores. Data moves between devices by JAX's collectives and lax.ppermute only.
A program may use at most 64 MiB of HBM per device.

```python
import jax
import jax.numpy as jnp
from jax import lax

DOFS = 192
MODES = 6
NAGG = 32
BLK_DEV = 16
SLOTS = 16
COARSE = 192
BLOCKS = 1024


def draw_neighbors(key, part):
    key = jax.random.fold_in(key, 11)
    row_ids = jnp.arange(BLOCKS, dtype=jnp.int32)
    slot_ids = jnp.arange(SLOTS, dtype=jnp.int32)
    offsets = jax.random.randint(key, (BLOCKS, SLOTS), -BLK_DEV, BLK_DEV + 1, dtype=jnp.int32)
    first_row = row_ids % BLK_DEV == 0
    last_row = row_ids % BLK_DEV == BLK_DEV - 1
    offsets = jnp.where(first_row[:, None] & (slot_ids == 0)[None, :], -BLK_DEV, offsets)
    offsets = jnp.where(last_row[:, None] & (slot_ids == 1)[None, :], BLK_DEV, offsets)
    return jnp.clip(row_ids[:, None] + offsets, 0, BLOCKS - 1).astype(jnp.int32)


def draw_live_counts(key, part):
    key = jax.random.fold_in(key, 23)
    row_ids = jnp.arange(BLOCKS, dtype=jnp.int32)
    counts = jax.random.randint(key, (BLOCKS,), SLOTS // 2, SLOTS + 1, dtype=jnp.int32)
    return jnp.where(row_ids % BLK_DEV == 0, SLOTS, counts).astype(jnp.int32)


def draw_prolong_aggs(key, part):
    key = jax.random.fold_in(key, 37)
    row_ids = jnp.arange(BLOCKS, dtype=jnp.int32)
    spots = jnp.arange(3 * BLK_DEV, dtype=jnp.int32)
    candidates = (row_ids // BLK_DEV - 1)[:, None] * BLK_DEV + spots[None, :]
    valid = (candidates >= 0) & (candidates < BLOCKS)
    noise = jax.random.randint(key, (BLOCKS, 3 * BLK_DEV), 0, 65536, dtype=jnp.int32)
    scores = noise * (4 * BLK_DEV) + spots[None, :]
    scores = jnp.where(candidates == row_ids[:, None], 131072 * (4 * BLK_DEV), scores)
    scores = jnp.where(valid, scores, -1 - spots[None, :])
    _, picks = lax.top_k(scores, NAGG)
    return jnp.take_along_axis(candidates, picks, axis=1).astype(jnp.int32)


def block_levels(rng, extent, split, low, top_value):
    def one(dim, parts):
        draws = jax.random.uniform(jax.random.fold_in(jax.random.fold_in(rng, 6), dim), (parts,), jnp.float32, low / len(split), top_value / len(split))
        return jnp.repeat(jnp.exp(draws), extent[dim] // parts).reshape((-1,) + (1,) * (len(extent) - dim - 1))

    gain = one(*split[0])
    for cut in split[1:]:
        gain = gain * one(*cut)
    return gain


def scatter_about(key, dims, width, most, cuts=(), kind=jnp.bfloat16):
    array = jax.random.normal(key, dims, jnp.float32) * width
    if len(cuts) > 0:
        array = block_levels(key, dims, cuts, -0.22, 0.18) * array
    return jnp.clip(array, min=-most, max=most).astype(kind)


def setup_inputs(seed: int = 0) -> dict:
    splits = jax.random.split(jax.random.key(seed), 6)
    stiffness = scatter_about(splits[0], (BLOCKS, SLOTS, DOFS, DOFS), DOFS ** -0.5, 0.4375, ((0, 64), (1, 4)))
    neighbors = draw_neighbors(jax.random.fold_in(splits[5], 71), 0)
    live_counts = draw_live_counts(jax.random.fold_in(splits[5], 71), 0)
    prolong = scatter_about(splits[3], (BLOCKS, COARSE, DOFS), 0.1, 0.59765625, ((0, 64), (1, 4)))
    prolong_aggs = draw_prolong_aggs(jax.random.fold_in(splits[5], 71), 0)
    return {"stiffness": stiffness, "neighbors": neighbors, "live_counts": live_counts, "prolong": prolong, "prolong_aggs": prolong_aggs}


def reference(stiffness, neighbors, live_counts, prolong, prolong_aggs):
    reach = 5 * BLK_DEV
    band = 7 * BLK_DEV

    def put_piece(piece, start):
        zero = jnp.int32(0)
        return lax.dynamic_update_slice(jnp.zeros((MODES, MODES, band), jnp.float32), piece, (zero, zero, start))

    def step(total, item):
        index, blocks, columns, count, own, groups = item
        home = (index // BLK_DEV).astype(jnp.int32)
        picked = jnp.take(prolong, columns, axis=0)
        image = jnp.einsum("kbf,kcf->kbc", blocks.astype(jnp.float32), picked.astype(jnp.float32))
        image = lax.optimization_barrier(image.astype(jnp.bfloat16)).astype(jnp.float32)
        live = jnp.arange(SLOTS, dtype=jnp.int32) < count
        image = jnp.where(live[:, None, None], image, jnp.zeros_like(image))
        far = (jnp.take(prolong_aggs, columns, axis=0) - (home - 2) * BLK_DEV).astype(jnp.int32)
        spread = image.reshape(SLOTS, DOFS, NAGG, MODES).transpose(1, 3, 0, 2).reshape(DOFS, MODES, SLOTS * NAGG)
        assembled = jnp.zeros((DOFS, MODES, reach), jnp.float32).at[:, :, far.reshape(-1)].add(spread)
        projected = jnp.dot(own.astype(jnp.float32), assembled.reshape(DOFS, MODES * reach), precision=lax.Precision.HIGHEST)
        projected = projected.reshape(NAGG, MODES, MODES, reach)
        starts = ((1 - (groups // BLK_DEV - home)) * BLK_DEV).astype(jnp.int32)
        placed = jax.vmap(put_piece)(projected, starts)
        return total.at[groups].add(placed), None

    start_total = jnp.zeros((BLOCKS, MODES, MODES, band), jnp.float32)
    items = (jnp.arange(BLOCKS, dtype=jnp.int32), stiffness, neighbors, live_counts, prolong, prolong_aggs)
    total, _ = lax.scan(step, start_total, items)
    return total.reshape(BLOCKS * MODES, MODES * band)
```

```python
import jax
import jax.numpy as jnp
from jax import lax
from jax.experimental import pallas as pl
from jax.experimental.pallas import tpu as pltpu
from jax.sharding import PartitionSpec as P

MODES = 6
LANES = 128
BF = jnp.bfloat16
F32 = jnp.float32


def from_behind(x, axis, by):
    length = lax.axis_size(axis)
    pairs = [(i, i + by) for i in range(length) if 0 <= i + by < length]
    return lax.ppermute(x, axis, pairs)


def around(x, axis, by):
    length = lax.axis_size(axis)
    return lax.ppermute(x, axis, [(i, (i + by) % length) for i in range(length)])


def pack_kernel(q_ref, out_ref):
    blocks, rows, _ = q_ref.shape
    half = blocks // 2
    groups = rows // MODES
    r = lax.broadcasted_iota(jnp.int32, (rows, rows), 0)
    c = lax.broadcasted_iota(jnp.int32, (rows, rows), 1)
    perm = jnp.where((r % groups) * MODES + r // groups == c, 1.0, 0.0).astype(BF)
    for j in range(half):
        a = jnp.dot(perm, q_ref[j], preferred_element_type=F32)
        b = jnp.dot(perm, q_ref[j + half], preferred_element_type=F32)
        out_ref[j * rows : (j + 1) * rows, :] = a[:, :LANES].astype(BF)
        out_ref[(j + half) * rows : (j + half + 1) * rows, :] = b[:, :LANES].astype(BF)
        mixed = jnp.concatenate([a[:, LANES:], b[:, LANES:]], axis=1)
        out_ref[(blocks + j) * rows : (blocks + j + 1) * rows, :] = mixed.astype(BF)


def main_kernel(
    pos_ref, aggr_ref, aggl_ref, s_hbm, w00, w01, w02, w03, below0, below, above0, above,
    low_ref, mid_ref, up_ref, wbuf, sbuf, acc, wsem, ssem
):
    blocks, slots, dofs, _ = sbuf.shape
    half = blocks // 2
    quarter = w00.shape[0]
    rows = quarter // (blocks + half)
    groups = rows // MODES
    parts = 4
    reach = 5 * blocks

    def window_copies():
        copies = []

        def add(src, place, count):
            copies.append(
                pltpu.make_async_copy(
                    src, wbuf.at[pl.ds(place * quarter, count * quarter)], wsem.at[len(copies)]
                )
            )

        add(below0, 0, 1)
        add(below, 1, 3)
        for d, own in enumerate((w00, w01, w02, w03)):
            add(own, parts + d, 1)
        add(above0, 2 * parts, 1)
        add(above, 2 * parts + 1, 3)
        return copies

    def stiff_copy(i):
        return pltpu.make_async_copy(s_hbm.at[i], sbuf.at[i], ssem.at[i])

    for cp in window_copies():
        cp.start()
    for n in range(half):
        stiff_copy(n).start()
        stiff_copy(n + half).start()
    acc[...] = jnp.zeros_like(acc)
    for cp in window_copies():
        cp.wait()

    def block_of(place, j):
        first = [
            wbuf[pl.ds(pl.multiple_of((place + d) * quarter + j * rows, 16), rows), :]
            for d in range(parts)
        ]
        jh = jnp.where(j >= half, j - half, j)
        second = [
            wbuf[pl.ds(pl.multiple_of((place + d) * quarter + (blocks + jh) * rows, 16), rows), :]
            for d in range(parts)
        ]
        return jnp.concatenate(
            [jnp.concatenate(first, axis=0), jnp.concatenate(second, axis=0)], axis=1
        )

    zeros = jnp.zeros((dofs, 2 * LANES - dofs), BF)

    def one(i, upper):
        images = []
        for k in range(slots):
            j = pos_ref[i * slots + k]
            w = j // blocks
            jl = j - w * blocks
            pj = block_of(w * parts, jl)
            s = sbuf[i, k]
            tail = s[:, LANES:]
            tail = jnp.where(
                jl < half,
                jnp.concatenate([tail, zeros], axis=1),
                jnp.concatenate([zeros, tail], axis=1),
            )
            sp = jnp.concatenate([s[:, :LANES], tail], axis=1)
            images.append(
                lax.dot_general(pj, sp, (((1,), (1,)), ((), ())), preferred_element_type=F32)
            )
        place_t = (
            lax.broadcasted_iota(jnp.int32, (reach, slots * parts * groups), 0)
            == aggr_ref[pl.ds(i, 1), :]
        )
        place_t = jnp.where(place_t, 1.0, 0.0).astype(BF)
        assembled = []
        for m in range(MODES):
            rhs = jnp.concatenate(
                [
                    img[d * rows + m * groups : d * rows + (m + 1) * groups]
                    for img in images
                    for d in range(parts)
                ],
                axis=0,
            ).astype(BF)
            assembled.append(jnp.dot(place_t, rhs, preferred_element_type=F32).astype(BF))
        assembled = jnp.concatenate(assembled, axis=0)
        hot = (
            lax.broadcasted_iota(jnp.int32, (3 * LANES, parts * rows), 0)
            == aggl_ref[pl.ds(i, 1), :]
        )
        hot = jnp.where(hot, 1.0, 0.0).astype(BF)
        left = jnp.dot(hot, block_of(parts, i), preferred_element_type=F32)
        if upper:
            left = jnp.concatenate([left[:, :LANES], left[:, dofs:]], axis=1)
        else:
            left = left[:, :dofs]
        return lax.dot_general(
            assembled, left.astype(BF), (((1,), (1,)), ((), ())), preferred_element_type=F32
        )

    def step(n, carry):
        stiff_copy(n).wait()
        stiff_copy(n + half).wait()
        acc[...] += one(n, False) + one(n + half, True)
        return carry

    lax.fori_loop(0, half, step, 0)
    width = low_ref.shape[1]
    low_ref[...] = acc[:, :width]
    mid_ref[...] = acc[:, LANES : LANES + width]
    up_ref[...] = acc[:, 2 * LANES : 2 * LANES + width]


def share_kernel(col_ref, mid_ref, above_ref, below_ref, o0, o1, o2, o3, tot):
    reach = mid_ref.shape[0] // MODES
    band = tot.shape[0] // MODES
    blocks = band // 7
    piece = o0.shape[0]
    tot[...] = jnp.zeros_like(tot)
    for m in range(MODES):
        src = slice(m * reach, (m + 1) * reach)
        tot[m * band + blocks : m * band + blocks + reach] += mid_ref[src]
        tot[m * band + 2 * blocks : m * band + 2 * blocks + reach] += above_ref[src]
        tot[m * band : m * band + reach] += below_ref[src]
    for d, o in enumerate((o0, o1, o2, o3)):
        c = col_ref[0] + d
        c = jnp.where(c >= 4, c - 4, c)
        o[...] = tot[pl.ds(pl.multiple_of(c * piece, 8), piece), :]


def final_kernel(a, b, c, d, out_ref):
    out_ref[...] = ((a[...] + b[...]) + (c[...] + d[...])).T


def on_device(stiffness, neighbors, live_counts, prolong, prolong_aggs):
    row_pos = lax.axis_index("rows")
    col_pos = lax.axis_index("cols")
    blocks, slots, dofs, _ = stiffness.shape
    rows = prolong.shape[1]
    groups = rows // MODES
    nagg = prolong_aggs.shape[1]
    parts = nagg // groups
    quarter = (blocks + blocks // 2) * rows
    vmem = pl.BlockSpec(memory_space=pltpu.VMEM)
    smem = pl.BlockSpec(memory_space=pltpu.SMEM)
    any_ = pl.BlockSpec(memory_space=pl.ANY)

    w0 = pl.pallas_call(
        pack_kernel,
        out_shape=jax.ShapeDtypeStruct((quarter, LANES), BF),
        in_specs=[vmem],
        out_specs=vmem,
    )(prolong)
    w1 = around(w0, "cols", -1)
    w3 = around(w0, "cols", 1)
    w2 = around(w0, "cols", 2)
    below0 = from_behind(w0, "rows", 1)
    above0 = from_behind(w0, "rows", -1)

    first_block = (row_pos - 1) * blocks
    pos = (neighbors - first_block).reshape(-1)
    cols_order = (col_pos + jnp.arange(parts, dtype=jnp.int32)) % parts
    rolled = jnp.take(prolong_aggs.reshape(-1, parts, groups), cols_order, axis=1)
    slot_global = col_pos * slots + jnp.arange(slots, dtype=jnp.int32)
    live = slot_global[None, :] < live_counts[:, None]
    far = jnp.take(rolled, neighbors.reshape(-1), axis=0).reshape(blocks, slots, parts * groups)
    aggr = jnp.where(live[:, :, None], far - (row_pos - 2) * blocks, -1)
    aggr = aggr.reshape(blocks, slots * nagg)
    own = lax.dynamic_slice_in_dim(rolled, row_pos * blocks, blocks, 0) - first_block
    own = (own // blocks) * LANES + (own % blocks) * MODES
    aggl = own[:, :, None, :] + jnp.arange(MODES, dtype=jnp.int32)[:, None]
    aggl = aggl.reshape(blocks, parts * rows)

    rest = jnp.concatenate([w1, w2, w3], axis=0)
    below = from_behind(rest, "rows", 1)
    above = from_behind(rest, "rows", -1)

    reach = 5 * blocks
    out = jax.ShapeDtypeStruct((MODES * reach, blocks * MODES), F32)
    low, mid, up = pl.pallas_call(
        main_kernel,
        out_shape=[out, out, out],
        in_specs=[smem, vmem, vmem] + [any_] * 9,
        out_specs=[vmem] * 3,
        scratch_shapes=[
            pltpu.VMEM((3 * parts * quarter, LANES), BF),
            pltpu.VMEM(stiffness.shape, BF),
            pltpu.VMEM((MODES * reach, 3 * LANES), F32),
            pltpu.SemaphoreType.DMA((8,)),
            pltpu.SemaphoreType.DMA((blocks,)),
        ],
        compiler_params=pltpu.CompilerParams(vmem_limit_bytes=40 * 2**20),
    )(pos, aggr, aggl, stiffness, w0, w1, w2, w3, below0, below, above0, above)
    from_above = from_behind(low, "rows", -1)
    from_below = from_behind(up, "rows", 1)
    piece = MODES * 7 * blocks // parts
    sh = jax.ShapeDtypeStruct((piece, blocks * MODES), F32)
    s0, s1, s2, s3 = pl.pallas_call(
        share_kernel,
        out_shape=[sh] * 4,
        in_specs=[smem] + [vmem] * 3,
        out_specs=[vmem] * 4,
        scratch_shapes=[pltpu.VMEM((MODES * 7 * blocks, blocks * MODES), F32)],
    )(col_pos.reshape(1), mid, from_above, from_below)
    t1 = around(s1, "cols", 1)
    t3 = around(s3, "cols", -1)
    t2 = around(s2, "cols", 2)
    return pl.pallas_call(
        final_kernel,
        out_shape=jax.ShapeDtypeStruct((blocks * MODES, piece), F32),
        in_specs=[vmem] * 4,
        out_specs=vmem,
    )(s0, t1, t2, t3)


def solution(mesh):
    in_specs = (
        P("rows", "cols", None, None),
        P("rows", "cols"),
        P("rows"),
        P("rows", "cols", None),
        P(),
    )
    out_specs = P("rows", "cols")
    return jax.shard_map(
        on_device, mesh=mesh, in_specs=in_specs, out_specs=out_specs, check_vma=False
    )
```

```python
import jax
import jax.numpy as jnp
from jax import lax
from jax.experimental import pallas as pl
from jax.experimental.pallas import tpu as pltpu
from jax.sharding import PartitionSpec as P

MODES = 6
LANES = 128
PARTS = 4
BF = jnp.bfloat16
F32 = jnp.float32
I32 = jnp.int32


def around(x, by):
    length = lax.axis_size("cols")
    return lax.ppermute(x, "cols", [(i, (i + by) % length) for i in range(length)])


def swap_chip(x):
    length = lax.axis_size("rows")
    return lax.ppermute(x, "rows", [(i, i ^ 1) for i in range(length)])


def swap_cross(x):
    rows = lax.axis_size("rows")
    cols = lax.axis_size("cols")
    pairs = []
    for c in range(cols):
        for r in range(1, rows - 1, 2):
            pairs += [(r * cols + c, (r + 1) * cols + c), ((r + 1) * cols + c, r * cols + c)]
        for r in (0, rows - 1):
            pairs.append((r * cols + c, r * cols + (c ^ 1)))
    return lax.ppermute(x, ("rows", "cols"), pairs)


def dot(a, b, trans_b=False):
    return lax.dot_general(
        a, b, (((1,), (1 if trans_b else 0,)), ((), ())), preferred_element_type=F32
    )


def pack_kernel(q_ref, out_ref):
    blocks, rows, dofs = q_ref.shape
    half = blocks // 2
    groups = rows // MODES
    many = 4
    r = lax.broadcasted_iota(I32, (many * rows, many * rows), 0)
    c = lax.broadcasted_iota(I32, (many * rows, many * rows), 1)
    rl = r % rows
    perm = (r - rl) + (rl % groups) * MODES + rl // groups == c
    perm = jnp.where(perm, 1.0, 0.0).astype(BF)
    step = many * rows
    for n in range(half // many):
        a = dot(perm, q_ref[n * many : (n + 1) * many].reshape(step, dofs))
        b = dot(perm, q_ref[half + n * many : half + (n + 1) * many].reshape(step, dofs))
        lo = n * step
        out_ref[lo : lo + step, :] = a[:, :LANES].astype(BF)
        hi = half * rows + lo
        out_ref[hi : hi + step, :] = b[:, :LANES].astype(BF)
        mixed = jnp.concatenate([a[:, LANES:], b[:, LANES:]], axis=1)
        tail = blocks * rows + lo
        out_ref[tail : tail + step, :] = mixed.astype(BF)


def table_kernel(where_ref, nbr_ref, aggs_ref, s_hbm, s_out, aggr_ref, aggl_ref, rel, ssem):
    slots, blocks = nbr_ref.shape
    copies = [pltpu.make_async_copy(s_hbm.at[i], s_out.at[i], ssem.at[i]) for i in range(blocks)]
    for cp in copies:
        cp.start()
    nagg, total = aggs_ref.shape
    groups = nagg // PARTS
    row = where_ref[0]
    col = where_ref[1]
    rel[...] = (aggs_ref[...] - (row - 2) * blocks).astype(F32)
    turned = []
    for d in range(PARTS):
        q = col + d
        q = jnp.where(q >= PARTS, q - PARTS, q)
        turned.append(rel[pl.ds(pl.multiple_of(q * groups, groups), groups), :])
    turned = jnp.concatenate(turned, axis=0).astype(BF)
    wanted = nbr_ref[...].T
    lane = lax.broadcasted_iota(I32, (blocks, total), 1)
    pieces = []
    for k in range(slots):
        hot = jnp.where(lane == wanted[:, k : k + 1], 1.0, 0.0).astype(BF)
        pieces.append(dot(hot, turned, True))
    aggr_ref[...] = jnp.concatenate(pieces, axis=1).astype(I32)
    sub = lax.broadcasted_iota(I32, (blocks, total), 0) + row * blocks
    own = dot(jnp.where(lane == sub, 1.0, 0.0).astype(BF), turned, True)
    src = lax.broadcasted_iota(I32, (nagg, MODES * nagg), 0)
    dst = lax.broadcasted_iota(I32, (nagg, MODES * nagg), 1)
    rows = MODES * groups
    spread = src == (dst // rows) * groups + dst % groups
    own = dot(own.astype(BF), jnp.where(spread, 1.0, 0.0).astype(BF)).astype(I32) - blocks
    mode = (lax.broadcasted_iota(I32, own.shape, 1) % rows) // groups
    aggl_ref[...] = (own // blocks) * LANES + (own % blocks) * MODES + mode
    for cp in copies:
        cp.wait()


def left_kernel(aggl_ref, w0, w1, w2, w3, out_ref):
    blocks = out_ref.shape[0]
    half = blocks // 2
    dofs = out_ref.shape[2]
    rows = aggl_ref.shape[1] // PARTS
    for i in range(blocks):
        hot = lax.broadcasted_iota(I32, (3 * LANES, PARTS * rows), 0) == aggl_ref[i : i + 1, :]
        hot = jnp.where(hot, 1.0, 0.0).astype(BF)
        first = jnp.concatenate([w[i * rows : (i + 1) * rows] for w in (w0, w1, w2, w3)], axis=0)
        at = (blocks + i % half) * rows
        second = jnp.concatenate([w[at : at + rows] for w in (w0, w1, w2, w3)], axis=0)
        left = dot(hot, jnp.concatenate([first, second], axis=1))
        if i < half:
            left = left[:, :dofs]
        else:
            left = jnp.concatenate([left[:, :LANES], left[:, dofs:]], axis=1)
        out_ref[i] = left.astype(BF)


def main_kernel(where_ref, nbr_ref, live_ref, aggr_ref, left_ref, sbuf, *rest):
    pieces = rest[: 3 * PARTS]
    chip_ref, mid_ref, cross_ref, wbuf, acc, wsem = rest[3 * PARTS :]
    blocks, slots, dofs, _ = sbuf.shape
    half = blocks // 2
    quarter = pieces[0].shape[0]
    rows = quarter // (blocks + half)
    groups = rows // MODES
    reach = 5 * blocks
    row = where_ref[0]
    col = where_ref[1]
    copies = [
        pltpu.make_async_copy(p, wbuf.at[pl.ds(n * quarter, quarter)], wsem.at[n])
        for n, p in enumerate(pieces)
    ]
    for cp in copies:
        cp.start()

    acc[...] = jnp.zeros_like(acc)
    zeros = jnp.zeros((dofs, 2 * LANES - dofs), BF)
    for cp in copies:
        cp.wait()

    def one(i):
        images = []
        for k in range(slots):
            j = nbr_ref[k, i] - (row - 1) * blocks
            w = j // blocks
            jl = j - w * blocks
            odd = row % 2
            w = jnp.where(w == 1, 0, jnp.where((w == 2) == (odd == 0), 1, 2))
            place = w * PARTS * quarter
            jh = jnp.where(jl >= half, jl - half, jl)
            first = [
                wbuf[pl.ds(pl.multiple_of(place + d * quarter + jl * rows, 16), rows), :]
                for d in range(PARTS)
            ]
            second = [
                wbuf[pl.ds(pl.multiple_of(place + d * quarter + (blocks + jh) * rows, 16), rows), :]
                for d in range(PARTS)
            ]
            pj = jnp.concatenate(
                [jnp.concatenate(first, axis=0), jnp.concatenate(second, axis=0)], axis=1
            )
            s = sbuf[i, k]
            tail = s[:, LANES:]
            tail = jnp.where(
                jl < half,
                jnp.concatenate([tail, zeros], axis=1),
                jnp.concatenate([zeros, tail], axis=1),
            )
            images.append(dot(pj, jnp.concatenate([s[:, :LANES], tail], axis=1), True))
        lane = lax.broadcasted_iota(I32, (1, slots * PARTS * groups), 1) // (PARTS * groups)
        target = jnp.where(lane + col * slots < live_ref[i], aggr_ref[pl.ds(i, 1), :], -1)
        place_t = lax.broadcasted_iota(I32, (reach, slots * PARTS * groups), 0) == target
        place_t = jnp.where(place_t, 1.0, 0.0).astype(BF)
        assembled = []
        for m in range(MODES):
            rhs = jnp.concatenate(
                [
                    img[d * rows + m * groups : d * rows + (m + 1) * groups]
                    for img in images
                    for d in range(PARTS)
                ],
                axis=0,
            ).astype(BF)
            assembled.append(dot(place_t, rhs).astype(BF))
        return dot(jnp.concatenate(assembled, axis=0), left_ref[i], True)

    def step(n, carry):
        acc[...] += one(n) + one(n + half)
        return carry

    lax.fori_loop(0, half, step, 0)
    width = mid_ref.shape[1]
    even = row % 2 == 0
    low = acc[:, :width]
    up = acc[:, 2 * LANES : 2 * LANES + width]
    chip_ref[...] = jnp.where(even, up, low)
    mid_ref[...] = acc[:, LANES : LANES + width]
    cross_ref[...] = jnp.where(even, low, up)


def share_kernel(where_ref, mid_ref, chip_ref, cross_ref, o0, o1, o2, o3, tot):
    reach = mid_ref.shape[0] // MODES
    band = tot.shape[0] // MODES
    blocks = band // 7
    piece = o0.shape[0]
    width = tot.shape[1]

    def zeros(n):
        return jnp.zeros((n * blocks, width), F32)

    even = where_ref[0] % 2 == 0
    for m in range(MODES):
        src = slice(m * reach, (m + 1) * reach)
        above = jnp.where(even, chip_ref[src], cross_ref[src])
        below = jnp.where(even, cross_ref[src], chip_ref[src])
        tot[m * band : (m + 1) * band] = (
            jnp.concatenate([zeros(1), mid_ref[src], zeros(1)], axis=0)
            + jnp.concatenate([zeros(2), above], axis=0)
            + jnp.concatenate([below, zeros(2)], axis=0)
        )
    for d, o in enumerate((o0, o1, o2, o3)):
        c = where_ref[1] + d
        c = jnp.where(c >= PARTS, c - PARTS, c)
        o[...] = tot[pl.ds(pl.multiple_of(c * piece, 8), piece), :]


def on_device(stiffness, neighbors, live_counts, prolong, prolong_aggs):
    row_pos = lax.axis_index("rows")
    col_pos = lax.axis_index("cols")
    blocks, slots, dofs, _ = stiffness.shape
    rows = prolong.shape[1]
    nagg = prolong_aggs.shape[1]
    quarter = (blocks + blocks // 2) * rows
    vmem = pl.BlockSpec(memory_space=pltpu.VMEM)
    smem = pl.BlockSpec(memory_space=pltpu.SMEM)
    any_ = pl.BlockSpec(memory_space=pl.ANY)
    hbm = pl.BlockSpec(memory_space=pltpu.HBM)
    where = jnp.stack([row_pos, col_pos]).astype(I32)
    nbr = neighbors.T

    w0 = pl.pallas_call(
        pack_kernel,
        out_shape=jax.ShapeDtypeStruct((quarter, LANES), BF),
        in_specs=[vmem],
        out_specs=vmem,
    )(prolong)
    w1 = around(w0, -1)
    w3 = around(w0, 1)
    b0 = swap_cross(w0)
    a0 = swap_chip(w0)
    later, a0 = lax.optimization_barrier((w0, a0))
    w2 = around(later, 2)

    s_near, aggr, aggl = pl.pallas_call(
        table_kernel,
        out_shape=[
            pltpu.VMEM(stiffness.shape, BF),
            jax.ShapeDtypeStruct((blocks, slots * nagg), I32),
            jax.ShapeDtypeStruct((blocks, MODES * nagg), I32),
        ],
        in_specs=[smem, vmem, vmem, hbm],
        out_specs=[vmem] * 3,
        scratch_shapes=[
            pltpu.VMEM((nagg, prolong_aggs.shape[0]), F32),
            pltpu.SemaphoreType.DMA((blocks,)),
        ],
        compiler_params=pltpu.CompilerParams(vmem_limit_bytes=52 * 2**20),
    )(where, nbr, prolong_aggs.T, stiffness)
    w1, w3, aggl = lax.optimization_barrier((w1, w3, aggl))

    b1 = swap_cross(w1)
    b3 = swap_cross(w3)
    a1 = swap_chip(w1)
    a3 = swap_chip(w3)
    w2, w1, w3 = lax.optimization_barrier((w2, w1, w3))
    b2 = swap_cross(w2)
    a2 = swap_chip(w2)

    left = pl.pallas_call(
        left_kernel,
        out_shape=pltpu.VMEM((blocks, 3 * LANES, dofs), BF),
        in_specs=[vmem] * 5,
        out_specs=vmem,
        compiler_params=pltpu.CompilerParams(vmem_limit_bytes=16 * 2**20),
    )(aggl, w0, w1, w2, w3)

    reach = 5 * blocks
    out = jax.ShapeDtypeStruct((MODES * reach, blocks * MODES), F32)
    to_chip, mid, to_cross = pl.pallas_call(
        main_kernel,
        out_shape=[out, out, out],
        in_specs=[smem, smem, smem, vmem, vmem, vmem] + [any_] * 12,
        out_specs=[vmem] * 3,
        scratch_shapes=[
            pltpu.VMEM((3 * PARTS * quarter, LANES), BF),
            pltpu.VMEM((MODES * reach, 3 * LANES), F32),
            pltpu.SemaphoreType.DMA((3 * PARTS,)),
        ],
        compiler_params=pltpu.CompilerParams(vmem_limit_bytes=40 * 2**20),
    )(where, nbr, live_counts, aggr, left, s_near, w0, w1, w2, w3, a0, a1, a2, a3, b0, b1, b2, b3)
    from_cross = swap_cross(to_cross)
    from_chip = swap_chip(to_chip)
    piece = MODES * 7 * blocks // PARTS
    sh = jax.ShapeDtypeStruct((piece, blocks * MODES), F32)
    s0, s1, s2, s3 = pl.pallas_call(
        share_kernel,
        out_shape=[sh] * 4,
        in_specs=[smem] + [vmem] * 3,
        out_specs=[vmem] * 4,
        scratch_shapes=[pltpu.VMEM((MODES * 7 * blocks, blocks * MODES), F32)],
    )(where, mid, from_chip, from_cross)
    t1 = around(s1, 1)
    t3 = around(s3, -1)
    t2 = around(s2, 2)
    return ((s0 + t1) + (t2 + t3)).T


def solution(mesh):
    in_specs = (
        P("rows", "cols", None, None),
        P("rows", "cols"),
        P("rows"),
        P("rows", "cols", None),
        P(),
    )
    out_specs = P("rows", "cols")
    return jax.shard_map(
        on_device, mesh=mesh, in_specs=in_specs, out_specs=out_specs, check_vma=False
    )
```

```python
import jax
import jax.numpy as jnp
from jax import lax
from jax.experimental import pallas as pl
from jax.experimental.pallas import tpu as pltpu
from jax.sharding import PartitionSpec as P

MODES = 6
LANES = 128
PARTS = 4
BF = jnp.bfloat16
F32 = jnp.float32
I32 = jnp.int32


def around(x, by):
    length = lax.axis_size("cols")
    return lax.ppermute(x, "cols", [(i, (i + by) % length) for i in range(length)])


def swap_chip(x):
    length = lax.axis_size("rows")
    return lax.ppermute(x, "rows", [(i, i ^ 1) for i in range(length)])


def swap_cross(x):
    rows = lax.axis_size("rows")
    cols = lax.axis_size("cols")
    pairs = []
    for c in range(cols):
        for r in range(1, rows - 1, 2):
            pairs += [(r * cols + c, (r + 1) * cols + c), ((r + 1) * cols + c, r * cols + c)]
        for r in (0, rows - 1):
            pairs.append((r * cols + c, r * cols + (c ^ 1)))
    return lax.ppermute(x, ("rows", "cols"), pairs)


def dot(a, b, trans_b=False):
    return lax.dot_general(
        a, b, (((1,), (1 if trans_b else 0,)), ((), ())), preferred_element_type=F32
    )


def pack_kernel(q_ref, out_ref):
    blocks, rows, dofs = q_ref.shape
    half = blocks // 2
    groups = rows // MODES
    many = 4
    r = lax.broadcasted_iota(I32, (many * rows, many * rows), 0)
    c = lax.broadcasted_iota(I32, (many * rows, many * rows), 1)
    rl = r % rows
    perm = (r - rl) + (rl % groups) * MODES + rl // groups == c
    perm = jnp.where(perm, 1.0, 0.0).astype(BF)
    step = many * rows
    for n in range(half // many):
        a = dot(perm, q_ref[n * many : (n + 1) * many].reshape(step, dofs))
        b = dot(perm, q_ref[half + n * many : half + (n + 1) * many].reshape(step, dofs))
        lo = n * step
        out_ref[lo : lo + step, :] = a[:, :LANES].astype(BF)
        hi = half * rows + lo
        out_ref[hi : hi + step, :] = b[:, :LANES].astype(BF)
        mixed = jnp.concatenate([a[:, LANES:], b[:, LANES:]], axis=1)
        tail = blocks * rows + lo
        out_ref[tail : tail + step, :] = mixed.astype(BF)


def table_kernel(nbr_ref, aggs_ref, s_hbm, s_out, aggr_ref, aggl_ref, rel, ssem):
    slots, blocks = nbr_ref.shape
    copies = [pltpu.make_async_copy(s_hbm.at[i], s_out.at[i], ssem.at[i]) for i in range(blocks)]
    for cp in copies:
        cp.start()
    nagg, total = aggs_ref.shape
    groups = nagg // PARTS
    row = lax.axis_index("rows")
    col = lax.axis_index("cols")
    rel[...] = (aggs_ref[...] - (row - 2) * blocks).astype(F32)
    turned = []
    for d in range(PARTS):
        q = col + d
        q = jnp.where(q >= PARTS, q - PARTS, q)
        turned.append(rel[pl.ds(pl.multiple_of(q * groups, groups), groups), :])
    turned = jnp.concatenate(turned, axis=0).astype(BF)
    wanted = nbr_ref[...].T
    lane = lax.broadcasted_iota(I32, (blocks, total), 1)
    pieces = []
    for k in range(slots):
        hot = jnp.where(lane == wanted[:, k : k + 1], 1.0, 0.0).astype(BF)
        pieces.append(dot(hot, turned, True))
    aggr_ref[...] = jnp.concatenate(pieces, axis=1).astype(I32)
    sub = lax.broadcasted_iota(I32, (blocks, total), 0) + row * blocks
    own = dot(jnp.where(lane == sub, 1.0, 0.0).astype(BF), turned, True)
    src = lax.broadcasted_iota(I32, (nagg, MODES * nagg), 0)
    dst = lax.broadcasted_iota(I32, (nagg, MODES * nagg), 1)
    rows = MODES * groups
    spread = src == (dst // rows) * groups + dst % groups
    own = dot(own.astype(BF), jnp.where(spread, 1.0, 0.0).astype(BF)).astype(I32) - blocks
    mode = (lax.broadcasted_iota(I32, own.shape, 1) % rows) // groups
    aggl_ref[...] = (own // blocks) * LANES + (own % blocks) * MODES + mode
    for cp in copies:
        cp.wait()


def left_kernel(aggl_ref, w0, w1, w2, w3, lo_ref, hi_ref):
    blocks = aggl_ref.shape[0]
    half = blocks // 2
    rows = aggl_ref.shape[1] // PARTS
    first_half = lax.broadcasted_iota(I32, (3 * LANES, LANES), 1) < LANES // 2

    def placed(i):
        hot = lax.broadcasted_iota(I32, (3 * LANES, PARTS * rows), 0) == aggl_ref[i : i + 1, :]
        hot = jnp.where(hot, 1.0, 0.0).astype(BF)
        first = jnp.concatenate([w[i * rows : (i + 1) * rows] for w in (w0, w1, w2, w3)], axis=0)
        at = (blocks + i % half) * rows
        second = jnp.concatenate([w[at : at + rows] for w in (w0, w1, w2, w3)], axis=0)
        left = dot(hot, jnp.concatenate([first, second], axis=1))
        lo_ref[:, i * LANES : (i + 1) * LANES] = left[:, :LANES].astype(BF)
        return left[:, LANES:]

    for n in range(half):
        a = placed(n)
        b = placed(n + half)
        hi_ref[:, n * LANES : (n + 1) * LANES] = jnp.where(first_half, a, b).astype(BF)


def main_kernel(nbr_ref, live_ref, aggr_ref, lo_ref, hi_ref, s_ref, *rest):
    pieces = rest[: 3 * PARTS]
    chip_ref, mid_ref, cross_ref, wbuf, images, asm_lo, asm_hi, wsem = rest[3 * PARTS :]
    blocks, slots, dofs, _ = s_ref.shape
    half = blocks // 2
    quarter = pieces[0].shape[0]
    rows = quarter // (blocks + half)
    groups = rows // MODES
    reach = 5 * blocks
    chunk = slots * PARTS * groups
    row = lax.axis_index("rows")
    col = lax.axis_index("cols")
    copies = [
        pltpu.make_async_copy(p, wbuf.at[pl.ds(n * quarter, quarter)], wsem.at[n])
        for n, p in enumerate(pieces)
    ]
    for cp in copies:
        cp.start()
    zeros = jnp.zeros((dofs, 2 * LANES - dofs), BF)
    odd = row % 2
    for cp in copies:
        cp.wait()

    def image(i, k):
        j = nbr_ref[k, i] - (row - 1) * blocks
        w = j // blocks
        jl = j - w * blocks
        w = jnp.where(w == 1, 0, jnp.where((w == 2) == (odd == 0), 1, 2))
        place = w * PARTS * quarter
        jh = jnp.where(jl >= half, jl - half, jl)
        first = [
            wbuf[pl.ds(pl.multiple_of(place + d * quarter + jl * rows, 16), rows), :]
            for d in range(PARTS)
        ]
        second = [
            wbuf[pl.ds(pl.multiple_of(place + d * quarter + (blocks + jh) * rows, 16), rows), :]
            for d in range(PARTS)
        ]
        pj = jnp.concatenate(
            [jnp.concatenate(first, axis=0), jnp.concatenate(second, axis=0)], axis=1
        )
        s = s_ref[i, k]
        tail = s[:, LANES:]
        tail = jnp.where(
            jl < half,
            jnp.concatenate([tail, zeros], axis=1),
            jnp.concatenate([zeros, tail], axis=1),
        )
        return dot(pj, jnp.concatenate([s[:, :LANES], tail], axis=1), True)

    for i in range(blocks):
        parts = [image(i, k) for k in range(slots)]
        for m in range(MODES):
            images[i, m * chunk : (m + 1) * chunk] = jnp.concatenate(
                [
                    img[d * rows + m * groups : d * rows + (m + 1) * groups]
                    for img in parts
                    for d in range(PARTS)
                ],
                axis=0,
            ).astype(BF)

    lane = lax.broadcasted_iota(I32, (1, chunk), 1) // (PARTS * groups)

    def assemble(i):
        target = jnp.where(lane + col * slots < live_ref[i], aggr_ref[i : i + 1, :], -1)
        place_t = lax.broadcasted_iota(I32, (reach, chunk), 0) == target
        place_t = jnp.where(place_t, 1.0, 0.0).astype(BF)
        tails = []
        for m in range(MODES):
            asm = dot(place_t, images[i, m * chunk : (m + 1) * chunk])
            asm_lo[m * reach : (m + 1) * reach, i * LANES : (i + 1) * LANES] = asm[
                :, :LANES
            ].astype(BF)
            tails.append(asm[:, LANES:].astype(BF))
        return tails

    for n in range(half):
        a = assemble(n)
        b = assemble(n + half)
        for m in range(MODES):
            asm_hi[m * reach : (m + 1) * reach, n * LANES : (n + 1) * LANES] = jnp.concatenate(
                [a[m], b[m]], axis=1
            )
    acc = dot(asm_lo[...], lo_ref[...], True) + dot(asm_hi[...], hi_ref[...], True)
    width = mid_ref.shape[1]
    even = odd == 0
    low = acc[:, :width]
    up = acc[:, 2 * LANES : 2 * LANES + width]
    chip_ref[...] = jnp.where(even, up, low)
    mid_ref[...] = acc[:, LANES : LANES + width]
    cross_ref[...] = jnp.where(even, low, up).astype(BF)


def share_kernel(mid_ref, chip_ref, cross_ref, o0, o1, o2, o3, tot):
    reach = mid_ref.shape[0] // MODES
    band = 7 * reach // 5
    blocks = band // 7
    piece = o0.shape[0]
    padded = o1.shape[0]
    width = tot.shape[1]

    def zeros(n):
        return jnp.zeros((n * blocks, width), F32)

    even = lax.axis_index("rows") % 2 == 0
    for m in range(MODES):
        src = slice(m * reach, (m + 1) * reach)
        chip = chip_ref[src]
        cross = cross_ref[src].astype(F32)
        above = jnp.where(even, chip, cross)
        below = jnp.where(even, cross, chip)
        tot[m * band : (m + 1) * band] = (
            jnp.concatenate([zeros(1), mid_ref[src], zeros(1)], axis=0)
            + jnp.concatenate([zeros(2), above], axis=0)
            + jnp.concatenate([below, zeros(2)], axis=0)
        )
    tot[MODES * band :] = jnp.zeros((padded - piece, width), F32)
    for d, o in enumerate((o0, o1, o2, o3)):
        c = lax.axis_index("cols") + d
        c = jnp.where(c >= PARTS, c - PARTS, c)
        o[...] = tot[pl.ds(pl.multiple_of(c * piece, 8), o.shape[0]), :].astype(o.dtype)


def on_device(stiffness, neighbors, live_counts, prolong, prolong_aggs):
    blocks, slots, dofs, _ = stiffness.shape
    rows = prolong.shape[1]
    nagg = prolong_aggs.shape[1]
    quarter = (blocks + blocks // 2) * rows
    vmem = pl.BlockSpec(memory_space=pltpu.VMEM)
    smem = pl.BlockSpec(memory_space=pltpu.SMEM)
    any_ = pl.BlockSpec(memory_space=pl.ANY)
    hbm = pl.BlockSpec(memory_space=pltpu.HBM)
    nbr = neighbors.T

    w0 = pl.pallas_call(
        pack_kernel,
        out_shape=jax.ShapeDtypeStruct((quarter, LANES), BF),
        in_specs=[vmem],
        out_specs=vmem,
        compiler_params=pltpu.CompilerParams(vmem_limit_bytes=8 * 2**20),
    )(prolong)
    w1 = around(w0, -1)
    w3 = around(w0, 1)
    b0 = swap_cross(w0)
    a0 = swap_chip(w0)
    aggs, a0 = lax.optimization_barrier((prolong_aggs.T, a0))
    w2 = around(w0, 2)

    s_near, aggr, aggl = pl.pallas_call(
        table_kernel,
        out_shape=[
            pltpu.VMEM(stiffness.shape, BF),
            pltpu.VMEM((blocks, slots * nagg), I32),
            pltpu.VMEM((blocks, MODES * nagg), I32),
        ],
        in_specs=[vmem, vmem, hbm],
        out_specs=[vmem] * 3,
        scratch_shapes=[
            pltpu.VMEM((nagg, prolong_aggs.shape[0]), F32),
            pltpu.SemaphoreType.DMA((blocks,)),
        ],
        compiler_params=pltpu.CompilerParams(vmem_limit_bytes=50 * 2**20),
    )(nbr, aggs, stiffness)
    w1, w3, aggl = lax.optimization_barrier((w1, w3, aggl))

    b1 = around(b0, -1)
    b3 = around(b0, 1)
    a1 = swap_chip(w1)
    a3 = swap_chip(w3)
    b2 = swap_cross(w2)
    a2 = swap_chip(w2)

    left_lo, left_hi = pl.pallas_call(
        left_kernel,
        out_shape=[
            pltpu.VMEM((3 * LANES, blocks * LANES), BF),
            pltpu.VMEM((3 * LANES, blocks * LANES // 2), BF),
        ],
        in_specs=[vmem] * 5,
        out_specs=[vmem] * 2,
        compiler_params=pltpu.CompilerParams(vmem_limit_bytes=16 * 2**20),
    )(aggl, w0, w1, w2, w3)

    reach = 5 * blocks
    out = jax.ShapeDtypeStruct((MODES * reach, blocks * MODES), F32)
    to_chip, mid, to_cross = pl.pallas_call(
        main_kernel,
        out_shape=[out, out, jax.ShapeDtypeStruct(out.shape, BF)],
        in_specs=[smem, smem, vmem, vmem, vmem, vmem] + [any_] * 12,
        out_specs=[vmem] * 3,
        scratch_shapes=[
            pltpu.VMEM((3 * PARTS * quarter, LANES), BF),
            pltpu.VMEM((blocks, slots * MODES * nagg, dofs), BF),
            pltpu.VMEM((MODES * reach, blocks * LANES), BF),
            pltpu.VMEM((MODES * reach, blocks * LANES // 2), BF),
            pltpu.SemaphoreType.DMA((3 * PARTS,)),
        ],
        compiler_params=pltpu.CompilerParams(vmem_limit_bytes=24 * 2**20),
    )(nbr, live_counts, aggr, left_lo, left_hi, s_near, w0, w1, w2, w3, a0, a1, a2, a3, b0, b1, b2, b3)
    from_cross = swap_cross(to_cross)
    from_chip = swap_chip(to_chip)
    piece = MODES * 7 * blocks // PARTS
    padded = -(-piece // 16) * 16
    sh = jax.ShapeDtypeStruct((padded, blocks * MODES), BF)
    s0, s1, s2, s3 = pl.pallas_call(
        share_kernel,
        out_shape=[jax.ShapeDtypeStruct((piece, blocks * MODES), F32), sh, sh, sh],
        in_specs=[vmem] * 3,
        out_specs=[vmem] * 4,
        scratch_shapes=[pltpu.VMEM((PARTS * piece + padded - piece, blocks * MODES), F32)],
        compiler_params=pltpu.CompilerParams(vmem_limit_bytes=8 * 2**20),
    )(mid, from_chip, from_cross)
    t1 = around(s1, 1)
    t3 = around(s3, -1)
    t2 = around(s2, 2)
    t1, t2, t3 = (t[:piece].astype(F32) for t in (t1, t2, t3))
    return ((s0 + t1) + (t2 + t3)).T


def solution(mesh):
    in_specs = (
        P("rows", "cols", None, None),
        P("rows", "cols"),
        P("rows"),
        P("rows", "cols", None),
        P(),
    )
    out_specs = P("rows", "cols")
    return jax.shard_map(
        on_device, mesh=mesh, in_specs=in_specs, out_specs=out_specs, check_vma=False
    )
```

```python
import jax
import jax.numpy as jnp
from jax import lax
from jax.experimental import pallas as pl
from jax.experimental.pallas import tpu as pltpu
from jax.sharding import PartitionSpec as P

MODES = 6
LANES = 128
PARTS = 4
BF = jnp.bfloat16
F32 = jnp.float32
I32 = jnp.int32


def around(x, by):
    length = lax.axis_size("cols")
    return lax.ppermute(x, "cols", [(i, (i + by) % length) for i in range(length)])


def swap_chip(x):
    length = lax.axis_size("rows")
    return lax.ppermute(x, "rows", [(i, i ^ 1) for i in range(length)])


def swap_cross(x):
    rows = lax.axis_size("rows")
    cols = lax.axis_size("cols")
    pairs = []
    for c in range(cols):
        for r in range(1, rows - 1, 2):
            pairs += [(r * cols + c, (r + 1) * cols + c), ((r + 1) * cols + c, r * cols + c)]
        for r in (0, rows - 1):
            pairs.append((r * cols + c, r * cols + (c ^ 1)))
    return lax.ppermute(x, ("rows", "cols"), pairs)


def dot(a, b, trans_b=False):
    return lax.dot_general(
        a, b, (((1,), (1 if trans_b else 0,)), ((), ())), preferred_element_type=F32
    )


def pack_kernel(q_ref, out_ref):
    blocks, rows, dofs = q_ref.shape
    half = blocks // 2
    groups = rows // MODES
    many = 4
    r = lax.broadcasted_iota(I32, (many * rows, many * rows), 0)
    c = lax.broadcasted_iota(I32, (many * rows, many * rows), 1)
    rl = r % rows
    perm = (r - rl) + (rl % groups) * MODES + rl // groups == c
    perm = jnp.where(perm, 1.0, 0.0).astype(BF)
    step = many * rows
    for n in range(half // many):
        a = dot(perm, q_ref[n * many : (n + 1) * many].reshape(step, dofs))
        b = dot(perm, q_ref[half + n * many : half + (n + 1) * many].reshape(step, dofs))
        lo = n * step
        out_ref[lo : lo + step, :] = a[:, :LANES].astype(BF)
        hi = half * rows + lo
        out_ref[hi : hi + step, :] = b[:, :LANES].astype(BF)
        mixed = jnp.concatenate([a[:, LANES:], b[:, LANES:]], axis=1)
        tail = blocks * rows + lo
        out_ref[tail : tail + step, :] = mixed.astype(BF)


def table_kernel(nbr_ref, aggs_ref, s_hbm, s_out, aggr_ref, aggl_ref, rel, ssem):
    slots, blocks = nbr_ref.shape
    copies = [pltpu.make_async_copy(s_hbm.at[i], s_out.at[i], ssem.at[i]) for i in range(blocks)]
    for cp in copies:
        cp.start()
    nagg, total = aggs_ref.shape
    groups = nagg // PARTS
    row = lax.axis_index("rows")
    col = lax.axis_index("cols")
    rel[...] = (aggs_ref[...] - (row - 2) * blocks).astype(F32)
    turned = []
    for d in range(PARTS):
        q = col + d
        q = jnp.where(q >= PARTS, q - PARTS, q)
        turned.append(rel[pl.ds(pl.multiple_of(q * groups, groups), groups), :])
    turned = jnp.concatenate(turned, axis=0).astype(BF)
    wanted = nbr_ref[...].T
    lane = lax.broadcasted_iota(I32, (blocks, total), 1)
    pieces = []
    for k in range(slots):
        hot = jnp.where(lane == wanted[:, k : k + 1], 1.0, 0.0).astype(BF)
        pieces.append(dot(hot, turned, True))
    aggr_ref[...] = jnp.concatenate(pieces, axis=1).astype(I32)
    sub = lax.broadcasted_iota(I32, (blocks, total), 0) + row * blocks
    own = dot(jnp.where(lane == sub, 1.0, 0.0).astype(BF), turned, True)
    src = lax.broadcasted_iota(I32, (nagg, MODES * nagg), 0)
    dst = lax.broadcasted_iota(I32, (nagg, MODES * nagg), 1)
    rows = MODES * groups
    spread = src == (dst // rows) * groups + dst % groups
    own = dot(own.astype(BF), jnp.where(spread, 1.0, 0.0).astype(BF)).astype(I32) - blocks
    mode = (lax.broadcasted_iota(I32, own.shape, 1) % rows) // groups
    aggl_ref[...] = (own // blocks) * LANES + (own % blocks) * MODES + mode
    for cp in copies:
        cp.wait()


def left_kernel(aggl_ref, w0, w1, w2, w3, lo_ref, hi_ref):
    blocks = aggl_ref.shape[0]
    half = blocks // 2
    rows = aggl_ref.shape[1] // PARTS
    first_half = lax.broadcasted_iota(I32, (3 * LANES, LANES), 1) < LANES // 2

    def placed(i):
        hot = lax.broadcasted_iota(I32, (3 * LANES, PARTS * rows), 0) == aggl_ref[i : i + 1, :]
        hot = jnp.where(hot, 1.0, 0.0).astype(BF)
        first = jnp.concatenate([w[i * rows : (i + 1) * rows] for w in (w0, w1, w2, w3)], axis=0)
        at = (blocks + i % half) * rows
        second = jnp.concatenate([w[at : at + rows] for w in (w0, w1, w2, w3)], axis=0)
        left = dot(hot, jnp.concatenate([first, second], axis=1))
        lo_ref[:, i * LANES : (i + 1) * LANES] = left[:, :LANES].astype(BF)
        return left[:, LANES:]

    for n in range(half):
        a = placed(n)
        b = placed(n + half)
        hi_ref[:, n * LANES : (n + 1) * LANES] = jnp.where(first_half, a, b).astype(BF)


def main_kernel(nbr_ref, live_ref, aggr_ref, lo_ref, hi_ref, s_ref, *rest):
    pieces = rest[: 3 * PARTS]
    chip_ref, mid_ref, cross_ref, wbuf, images, asm_lo, asm_hi, wsem = rest[3 * PARTS :]
    blocks, slots, dofs, _ = s_ref.shape
    half = blocks // 2
    quarter = pieces[0].shape[0]
    rows = quarter // (blocks + half)
    groups = rows // MODES
    reach = 5 * blocks
    chunk = slots * PARTS * groups
    row = lax.axis_index("rows")
    col = lax.axis_index("cols")
    copies = [
        pltpu.make_async_copy(p, wbuf.at[pl.ds(n * quarter, quarter)], wsem.at[n])
        for n, p in enumerate(pieces)
    ]
    for cp in copies:
        cp.start()
    zeros = jnp.zeros((dofs, 2 * LANES - dofs), BF)
    odd = row % 2
    for cp in copies:
        cp.wait()

    def image(i, k):
        j = nbr_ref[k, i] - (row - 1) * blocks
        w = j // blocks
        jl = j - w * blocks
        w = jnp.where(w == 1, 0, jnp.where((w == 2) == (odd == 0), 1, 2))
        place = w * PARTS * quarter
        jh = jnp.where(jl >= half, jl - half, jl)
        first = [
            wbuf[pl.ds(pl.multiple_of(place + d * quarter + jl * rows, 16), rows), :]
            for d in range(PARTS)
        ]
        second = [
            wbuf[pl.ds(pl.multiple_of(place + d * quarter + (blocks + jh) * rows, 16), rows), :]
            for d in range(PARTS)
        ]
        pj = jnp.concatenate(
            [jnp.concatenate(first, axis=0), jnp.concatenate(second, axis=0)], axis=1
        )
        s = s_ref[i, k]
        tail = s[:, LANES:]
        tail = jnp.where(
            jl < half,
            jnp.concatenate([tail, zeros], axis=1),
            jnp.concatenate([zeros, tail], axis=1),
        )
        return dot(pj, jnp.concatenate([s[:, :LANES], tail], axis=1), True)

    for i in range(blocks):
        parts = [image(i, k) for k in range(slots)]
        for m in range(MODES):
            images[i, m * chunk : (m + 1) * chunk] = jnp.concatenate(
                [
                    img[d * rows + m * groups : d * rows + (m + 1) * groups]
                    for img in parts
                    for d in range(PARTS)
                ],
                axis=0,
            ).astype(BF)

    lane = lax.broadcasted_iota(I32, (1, chunk), 1) // (PARTS * groups)

    def assemble(i):
        target = jnp.where(lane + col * slots < live_ref[i], aggr_ref[i : i + 1, :], -1)
        place_t = lax.broadcasted_iota(I32, (reach, chunk), 0) == target
        place_t = jnp.where(place_t, 1.0, 0.0).astype(BF)
        tails = []
        for m in range(MODES):
            asm = dot(place_t, images[i, m * chunk : (m + 1) * chunk])
            asm_lo[m * reach : (m + 1) * reach, i * LANES : (i + 1) * LANES] = asm[
                :, :LANES
            ].astype(BF)
            tails.append(asm[:, LANES:].astype(BF))
        return tails

    for n in range(half):
        a = assemble(n)
        b = assemble(n + half)
        for m in range(MODES):
            asm_hi[m * reach : (m + 1) * reach, n * LANES : (n + 1) * LANES] = jnp.concatenate(
                [a[m], b[m]], axis=1
            )
    acc = dot(asm_lo[...], lo_ref[...], True) + dot(asm_hi[...], hi_ref[...], True)
    width = mid_ref.shape[1]
    even = odd == 0
    low = acc[:, :width]
    up = acc[:, 2 * LANES : 2 * LANES + width]
    chip_ref[...] = jnp.where(even, up, low)
    mid_ref[...] = acc[:, LANES : LANES + width]
    cross_ref[...] = jnp.where(even, low, up).astype(BF)


def share_kernel(mid_ref, chip_ref, cross_ref, o0, o1, o2, o3, tot):
    reach = mid_ref.shape[0] // MODES
    band = 7 * reach // 5
    blocks = band // 7
    piece = o0.shape[0]
    padded = o1.shape[0]
    width = tot.shape[1]

    def zeros(n):
        return jnp.zeros((n * blocks, width), F32)

    even = lax.axis_index("rows") % 2 == 0
    for m in range(MODES):
        src = slice(m * reach, (m + 1) * reach)
        chip = chip_ref[src]
        cross = cross_ref[src].astype(F32)
        above = jnp.where(even, chip, cross)
        below = jnp.where(even, cross, chip)
        tot[m * band : (m + 1) * band] = (
            jnp.concatenate([zeros(1), mid_ref[src], zeros(1)], axis=0)
            + jnp.concatenate([zeros(2), above], axis=0)
            + jnp.concatenate([below, zeros(2)], axis=0)
        )
    tot[MODES * band :] = jnp.zeros((padded - piece, width), F32)
    for d, o in enumerate((o0, o1, o2, o3)):
        c = lax.axis_index("cols") + d
        c = jnp.where(c >= PARTS, c - PARTS, c)
        o[...] = tot[pl.ds(pl.multiple_of(c * piece, 8), o.shape[0]), :].astype(o.dtype)


def on_device(stiffness, neighbors, live_counts, prolong, prolong_aggs):
    blocks, slots, dofs, _ = stiffness.shape
    rows = prolong.shape[1]
    nagg = prolong_aggs.shape[1]
    quarter = (blocks + blocks // 2) * rows
    vmem = pl.BlockSpec(memory_space=pltpu.VMEM)
    smem = pl.BlockSpec(memory_space=pltpu.SMEM)
    any_ = pl.BlockSpec(memory_space=pl.ANY)
    hbm = pl.BlockSpec(memory_space=pltpu.HBM)
    nbr = neighbors.T

    w0 = pl.pallas_call(
        pack_kernel,
        out_shape=jax.ShapeDtypeStruct((quarter, LANES), BF),
        in_specs=[vmem],
        out_specs=vmem,
        compiler_params=pltpu.CompilerParams(vmem_limit_bytes=8 * 2**20),
    )(prolong)
    w2 = around(w0, 2)
    w1 = around(w0, -1)
    w3 = around(w0, 1)
    b0 = swap_cross(w0)
    aggs, b0 = lax.optimization_barrier((prolong_aggs.T, b0))

    s_near, aggr, aggl = pl.pallas_call(
        table_kernel,
        out_shape=[
            pltpu.VMEM(stiffness.shape, BF),
            pltpu.VMEM((blocks, slots * nagg), I32),
            pltpu.VMEM((blocks, MODES * nagg), I32),
        ],
        in_specs=[vmem, vmem, hbm],
        out_specs=[vmem] * 3,
        scratch_shapes=[
            pltpu.VMEM((nagg, prolong_aggs.shape[0]), F32),
            pltpu.SemaphoreType.DMA((blocks,)),
        ],
        compiler_params=pltpu.CompilerParams(vmem_limit_bytes=50 * 2**20),
    )(nbr, aggs, stiffness)
    w2, aggl = lax.optimization_barrier((w2, aggl))

    b1 = around(b0, -1)
    b3 = around(b0, 1)
    b2 = swap_cross(w2)
    q1, q3, b1 = lax.optimization_barrier((w1, w3, b1))
    a0, a1, a2, a3 = (swap_chip(q) for q in (w0, q1, w2, q3))

    left_lo, left_hi = pl.pallas_call(
        left_kernel,
        out_shape=[
            pltpu.VMEM((3 * LANES, blocks * LANES), BF),
            pltpu.VMEM((3 * LANES, blocks * LANES // 2), BF),
        ],
        in_specs=[vmem] * 5,
        out_specs=[vmem] * 2,
        compiler_params=pltpu.CompilerParams(vmem_limit_bytes=16 * 2**20),
    )(aggl, w0, w1, w2, w3)

    reach = 5 * blocks
    out = jax.ShapeDtypeStruct((MODES * reach, blocks * MODES), F32)
    to_chip, mid, to_cross = pl.pallas_call(
        main_kernel,
        out_shape=[out, out, jax.ShapeDtypeStruct(out.shape, BF)],
        in_specs=[smem, smem, vmem, vmem, vmem, vmem] + [any_] * 12,
        out_specs=[vmem] * 3,
        scratch_shapes=[
            pltpu.VMEM((3 * PARTS * quarter, LANES), BF),
            pltpu.VMEM((blocks, slots * MODES * nagg, dofs), BF),
            pltpu.VMEM((MODES * reach, blocks * LANES), BF),
            pltpu.VMEM((MODES * reach, blocks * LANES // 2), BF),
            pltpu.SemaphoreType.DMA((3 * PARTS,)),
        ],
        compiler_params=pltpu.CompilerParams(vmem_limit_bytes=24 * 2**20),
    )(nbr, live_counts, aggr, left_lo, left_hi, s_near, w0, w1, w2, w3, a0, a1, a2, a3, b0, b1, b2, b3)
    from_cross = swap_cross(to_cross)
    from_chip = swap_chip(to_chip)
    piece = MODES * 7 * blocks // PARTS
    padded = -(-piece // 16) * 16
    sh = jax.ShapeDtypeStruct((padded, blocks * MODES), BF)
    s0, s1, s2, s3 = pl.pallas_call(
        share_kernel,
        out_shape=[jax.ShapeDtypeStruct((piece, blocks * MODES), F32), sh, sh, sh],
        in_specs=[vmem] * 3,
        out_specs=[vmem] * 4,
        scratch_shapes=[pltpu.VMEM((PARTS * piece + padded - piece, blocks * MODES), F32)],
        compiler_params=pltpu.CompilerParams(vmem_limit_bytes=8 * 2**20),
    )(mid, from_chip, from_cross)
    t1 = around(s1, 1)
    t3 = around(s3, -1)
    t2 = around(s2, 2)
    t1, t2, t3 = (t[:piece].astype(F32) for t in (t1, t2, t3))
    return ((s0 + t1) + (t2 + t3)).T


def solution(mesh):
    in_specs = (
        P("rows", "cols", None, None),
        P("rows", "cols"),
        P("rows"),
        P("rows", "cols", None),
        P(),
    )
    out_specs = P("rows", "cols")
    return jax.shard_map(
        on_device, mesh=mesh, in_specs=in_specs, out_specs=out_specs, check_vma=False
    )
```

```python
import jax
import jax.numpy as jnp
from jax import lax
from jax.experimental import pallas as pl
from jax.experimental.pallas import tpu as pltpu
from jax.sharding import PartitionSpec as P

MODES = 6
LANES = 128
PARTS = 4
BF = jnp.bfloat16
F32 = jnp.float32
I32 = jnp.int32


def around(x, by):
    length = lax.axis_size("cols")
    return lax.ppermute(x, "cols", [(i, (i + by) % length) for i in range(length)])


def swap_chip(x):
    length = lax.axis_size("rows")
    return lax.ppermute(x, "rows", [(i, i ^ 1) for i in range(length)])


def swap_cross(x, turn=1):
    rows = lax.axis_size("rows")
    cols = lax.axis_size("cols")
    pairs = []
    for c in range(cols):
        for r in range(1, rows - 1, 2):
            pairs += [(r * cols + c, (r + 1) * cols + c), ((r + 1) * cols + c, r * cols + c)]
        for r in (0, rows - 1):
            pairs.append((r * cols + c, r * cols + (c ^ turn)))
    return lax.ppermute(x, ("rows", "cols"), pairs)


def dot(a, b, trans_b=False):
    return lax.dot_general(
        a, b, (((1,), (1 if trans_b else 0,)), ((), ())), preferred_element_type=F32
    )


def pack_kernel(q_ref, out_ref):
    blocks, rows, dofs = q_ref.shape
    half = blocks // 2
    groups = rows // MODES
    many = 4
    r = lax.broadcasted_iota(I32, (many * rows, many * rows), 0)
    c = lax.broadcasted_iota(I32, (many * rows, many * rows), 1)
    rl = r % rows
    perm = (r - rl) + (rl % groups) * MODES + rl // groups == c
    perm = jnp.where(perm, 1.0, 0.0).astype(BF)
    step = many * rows
    for n in range(half // many):
        a = dot(perm, q_ref[n * many : (n + 1) * many].reshape(step, dofs))
        b = dot(perm, q_ref[half + n * many : half + (n + 1) * many].reshape(step, dofs))
        lo = n * step
        out_ref[lo : lo + step, :] = a[:, :LANES].astype(BF)
        hi = half * rows + lo
        out_ref[hi : hi + step, :] = b[:, :LANES].astype(BF)
        mixed = jnp.concatenate([a[:, LANES:], b[:, LANES:]], axis=1)
        tail = blocks * rows + lo
        out_ref[tail : tail + step, :] = mixed.astype(BF)


def table_kernel(nbr_ref, aggs_ref, s_hbm, s_out, aggr_ref, aggl_ref, rel, ssem):
    slots, blocks = nbr_ref.shape
    copies = [pltpu.make_async_copy(s_hbm.at[i], s_out.at[i], ssem.at[i]) for i in range(blocks)]
    for cp in copies:
        cp.start()
    nagg, total = aggs_ref.shape
    groups = nagg // PARTS
    row = lax.axis_index("rows")
    col = lax.axis_index("cols")
    rel[...] = (aggs_ref[...] - (row - 2) * blocks).astype(F32)
    turned = []
    for d in range(PARTS):
        q = col + d
        q = jnp.where(q >= PARTS, q - PARTS, q)
        turned.append(rel[pl.ds(pl.multiple_of(q * groups, groups), groups), :])
    turned = jnp.concatenate(turned, axis=0).astype(BF)
    wanted = nbr_ref[...].T
    lane = lax.broadcasted_iota(I32, (blocks, total), 1)
    pieces = []
    for k in range(slots):
        hot = jnp.where(lane == wanted[:, k : k + 1], 1.0, 0.0).astype(BF)
        pieces.append(dot(hot, turned, True))
    aggr_ref[...] = jnp.concatenate(pieces, axis=1).astype(I32)
    sub = lax.broadcasted_iota(I32, (blocks, total), 0) + row * blocks
    own = dot(jnp.where(lane == sub, 1.0, 0.0).astype(BF), turned, True)
    src = lax.broadcasted_iota(I32, (nagg, MODES * nagg), 0)
    dst = lax.broadcasted_iota(I32, (nagg, MODES * nagg), 1)
    rows = MODES * groups
    spread = src == (dst // rows) * groups + dst % groups
    own = dot(own.astype(BF), jnp.where(spread, 1.0, 0.0).astype(BF)).astype(I32) - blocks
    mode = (lax.broadcasted_iota(I32, own.shape, 1) % rows) // groups
    aggl_ref[...] = (own // blocks) * LANES + (own % blocks) * MODES + mode
    for cp in copies:
        cp.wait()


def left_kernel(aggl_ref, w0, w1, w2, w3, lo_ref, hi_ref):
    blocks = aggl_ref.shape[0]
    half = blocks // 2
    rows = aggl_ref.shape[1] // PARTS
    first_half = lax.broadcasted_iota(I32, (3 * LANES, LANES), 1) < LANES // 2

    def placed(i):
        hot = lax.broadcasted_iota(I32, (3 * LANES, PARTS * rows), 0) == aggl_ref[i : i + 1, :]
        hot = jnp.where(hot, 1.0, 0.0).astype(BF)
        first = jnp.concatenate([w[i * rows : (i + 1) * rows] for w in (w0, w1, w2, w3)], axis=0)
        at = (blocks + i % half) * rows
        second = jnp.concatenate([w[at : at + rows] for w in (w0, w1, w2, w3)], axis=0)
        left = dot(hot, jnp.concatenate([first, second], axis=1))
        lo_ref[:, i * LANES : (i + 1) * LANES] = left[:, :LANES].astype(BF)
        return left[:, LANES:]

    for n in range(half):
        a = placed(n)
        b = placed(n + half)
        hi_ref[:, n * LANES : (n + 1) * LANES] = jnp.where(first_half, a, b).astype(BF)


def main_kernel(nbr_ref, live_ref, aggr_ref, lo_ref, hi_ref, s_ref, *rest):
    pieces = rest[: 3 * PARTS]
    chip_ref, mid_ref, cross_ref, wbuf, images, asm_lo, asm_hi, wsem = rest[3 * PARTS :]
    blocks, slots, dofs, _ = s_ref.shape
    half = blocks // 2
    quarter = pieces[0].shape[0]
    rows = quarter // (blocks + half)
    groups = rows // MODES
    reach = 5 * blocks
    chunk = slots * PARTS * groups
    row = lax.axis_index("rows")
    col = lax.axis_index("cols")
    copies = [
        pltpu.make_async_copy(p, wbuf.at[pl.ds(n * quarter, quarter)], wsem.at[n])
        for n, p in enumerate(pieces)
    ]
    for cp in copies:
        cp.start()
    zeros = jnp.zeros((dofs, 2 * LANES - dofs), BF)
    odd = row % 2
    for cp in copies:
        cp.wait()

    def image(i, k):
        j = nbr_ref[k, i] - (row - 1) * blocks
        w = j // blocks
        jl = j - w * blocks
        w = jnp.where(w == 1, 0, jnp.where((w == 2) == (odd == 0), 1, 2))
        place = w * PARTS * quarter
        jh = jnp.where(jl >= half, jl - half, jl)
        first = [
            wbuf[pl.ds(pl.multiple_of(place + d * quarter + jl * rows, 16), rows), :]
            for d in range(PARTS)
        ]
        second = [
            wbuf[pl.ds(pl.multiple_of(place + d * quarter + (blocks + jh) * rows, 16), rows), :]
            for d in range(PARTS)
        ]
        pj = jnp.concatenate(
            [jnp.concatenate(first, axis=0), jnp.concatenate(second, axis=0)], axis=1
        )
        s = s_ref[i, k]
        tail = s[:, LANES:]
        tail = jnp.where(
            jl < half,
            jnp.concatenate([tail, zeros], axis=1),
            jnp.concatenate([zeros, tail], axis=1),
        )
        return dot(pj, jnp.concatenate([s[:, :LANES], tail], axis=1), True)

    for i in range(blocks):
        parts = [image(i, k) for k in range(slots)]
        for m in range(MODES):
            images[i, m * chunk : (m + 1) * chunk] = jnp.concatenate(
                [
                    img[d * rows + m * groups : d * rows + (m + 1) * groups]
                    for img in parts
                    for d in range(PARTS)
                ],
                axis=0,
            ).astype(BF)

    lane = lax.broadcasted_iota(I32, (1, chunk), 1) // (PARTS * groups)

    def assemble(i):
        target = jnp.where(lane + col * slots < live_ref[i], aggr_ref[i : i + 1, :], -1)
        place_t = lax.broadcasted_iota(I32, (reach, chunk), 0) == target
        place_t = jnp.where(place_t, 1.0, 0.0).astype(BF)
        tails = []
        for m in range(MODES):
            asm = dot(place_t, images[i, m * chunk : (m + 1) * chunk])
            asm_lo[m * reach : (m + 1) * reach, i * LANES : (i + 1) * LANES] = asm[
                :, :LANES
            ].astype(BF)
            tails.append(asm[:, LANES:].astype(BF))
        return tails

    for n in range(half):
        a = assemble(n)
        b = assemble(n + half)
        for m in range(MODES):
            asm_hi[m * reach : (m + 1) * reach, n * LANES : (n + 1) * LANES] = jnp.concatenate(
                [a[m], b[m]], axis=1
            )
    acc = dot(asm_lo[...], lo_ref[...], True) + dot(asm_hi[...], hi_ref[...], True)
    width = mid_ref.shape[1]
    even = odd == 0
    low = acc[:, :width]
    up = acc[:, 2 * LANES : 2 * LANES + width]
    chip_ref[...] = jnp.where(even, up, low)
    mid_ref[...] = acc[:, LANES : LANES + width]
    cross_ref[...] = jnp.where(even, low, up).astype(BF)


def share_kernel(mid_ref, chip_ref, cross_ref, o0, o1, o2, o3, tot):
    reach = mid_ref.shape[0] // MODES
    band = 7 * reach // 5
    blocks = band // 7
    piece = o0.shape[0]
    padded = o1.shape[0]
    width = tot.shape[1]

    def zeros(n):
        return jnp.zeros((n * blocks, width), F32)

    even = lax.axis_index("rows") % 2 == 0
    for m in range(MODES):
        src = slice(m * reach, (m + 1) * reach)
        chip = chip_ref[src]
        cross = cross_ref[src].astype(F32)
        above = jnp.where(even, chip, cross)
        below = jnp.where(even, cross, chip)
        tot[m * band : (m + 1) * band] = (
            jnp.concatenate([zeros(1), mid_ref[src], zeros(1)], axis=0)
            + jnp.concatenate([zeros(2), above], axis=0)
            + jnp.concatenate([below, zeros(2)], axis=0)
        )
    tot[MODES * band :] = jnp.zeros((padded - piece, width), F32)
    for d, o in enumerate((o0, o1, o2, o3)):
        c = lax.axis_index("cols") + d
        c = jnp.where(c >= PARTS, c - PARTS, c)
        o[...] = tot[pl.ds(pl.multiple_of(c * piece, 8), o.shape[0]), :].astype(o.dtype)


def on_device(stiffness, neighbors, live_counts, prolong, prolong_aggs):
    blocks, slots, dofs, _ = stiffness.shape
    rows = prolong.shape[1]
    nagg = prolong_aggs.shape[1]
    quarter = (blocks + blocks // 2) * rows
    vmem = pl.BlockSpec(memory_space=pltpu.VMEM)
    smem = pl.BlockSpec(memory_space=pltpu.SMEM)
    any_ = pl.BlockSpec(memory_space=pl.ANY)
    hbm = pl.BlockSpec(memory_space=pltpu.HBM)
    nbr = neighbors.T

    w0 = pl.pallas_call(
        pack_kernel,
        out_shape=jax.ShapeDtypeStruct((quarter, LANES), BF),
        in_specs=[vmem],
        out_specs=vmem,
        compiler_params=pltpu.CompilerParams(vmem_limit_bytes=8 * 2**20),
    )(prolong)
    w2 = around(w0, 2)
    w1 = around(w0, -1)
    w3 = around(w0, 1)
    b0 = swap_cross(w0)
    aggs = prolong_aggs.T

    s_near, aggr, aggl = pl.pallas_call(
        table_kernel,
        out_shape=[
            pltpu.VMEM(stiffness.shape, BF),
            pltpu.VMEM((blocks, slots * nagg), I32),
            pltpu.VMEM((blocks, MODES * nagg), I32),
        ],
        in_specs=[vmem, vmem, hbm],
        out_specs=[vmem] * 3,
        scratch_shapes=[
            pltpu.VMEM((nagg, prolong_aggs.shape[0]), F32),
            pltpu.SemaphoreType.DMA((blocks,)),
        ],
        compiler_params=pltpu.CompilerParams(vmem_limit_bytes=50 * 2**20),
    )(nbr, aggs, stiffness)
    w2, aggl = lax.optimization_barrier((w2, aggl))

    b1 = around(b0, -1)
    b3 = around(b0, 1)
    b2 = swap_cross(w2, 3)
    q0, q1, q2, q3, b2 = lax.optimization_barrier((w0, w1, w2, w3, b2))
    a0, a1, a2, a3 = (swap_chip(q) for q in (q0, q1, q2, q3))

    left_lo, left_hi = pl.pallas_call(
        left_kernel,
        out_shape=[
            pltpu.VMEM((3 * LANES, blocks * LANES), BF),
            pltpu.VMEM((3 * LANES, blocks * LANES // 2), BF),
        ],
        in_specs=[vmem] * 5,
        out_specs=[vmem] * 2,
        compiler_params=pltpu.CompilerParams(vmem_limit_bytes=16 * 2**20),
    )(aggl, w0, w1, w2, w3)

    reach = 5 * blocks
    out = jax.ShapeDtypeStruct((MODES * reach, blocks * MODES), F32)
    to_chip, mid, to_cross = pl.pallas_call(
        main_kernel,
        out_shape=[out, out, jax.ShapeDtypeStruct(out.shape, BF)],
        in_specs=[smem, smem, vmem, vmem, vmem, vmem] + [any_] * 12,
        out_specs=[vmem] * 3,
        scratch_shapes=[
            pltpu.VMEM((3 * PARTS * quarter, LANES), BF),
            pltpu.VMEM((blocks, slots * MODES * nagg, dofs), BF),
            pltpu.VMEM((MODES * reach, blocks * LANES), BF),
            pltpu.VMEM((MODES * reach, blocks * LANES // 2), BF),
            pltpu.SemaphoreType.DMA((3 * PARTS,)),
        ],
        compiler_params=pltpu.CompilerParams(vmem_limit_bytes=24 * 2**20),
    )(nbr, live_counts, aggr, left_lo, left_hi, s_near, w0, w1, w2, w3, a0, a1, a2, a3, b0, b1, b2, b3)
    from_cross = swap_cross(to_cross)
    from_chip = swap_chip(to_chip)
    piece = MODES * 7 * blocks // PARTS
    padded = -(-piece // 16) * 16
    sh = jax.ShapeDtypeStruct((padded, blocks * MODES), BF)
    s0, s1, s2, s3 = pl.pallas_call(
        share_kernel,
        out_shape=[jax.ShapeDtypeStruct((piece, blocks * MODES), F32), sh, sh, sh],
        in_specs=[vmem] * 3,
        out_specs=[vmem] * 4,
        scratch_shapes=[pltpu.VMEM((PARTS * piece + padded - piece, blocks * MODES), F32)],
        compiler_params=pltpu.CompilerParams(vmem_limit_bytes=8 * 2**20),
    )(mid, from_chip, from_cross)
    t1 = around(s1, 1)
    t3 = around(s3, -1)
    t2 = around(s2, 2)
    t1, t2, t3 = (t[:piece].astype(F32) for t in (t1, t2, t3))
    return ((s0 + t1) + (t2 + t3)).T


def solution(mesh):
    in_specs = (
        P("rows", "cols", None, None),
        P("rows", "cols"),
        P("rows"),
        P("rows", "cols", None),
        P(),
    )
    out_specs = P("rows", "cols")
    return jax.shard_map(
        on_device, mesh=mesh, in_specs=in_specs, out_specs=out_specs, check_vma=False
    )
```

```python
import jax
import jax.numpy as jnp
from jax import lax
from jax.experimental import pallas as pl
from jax.experimental.pallas import tpu as pltpu
from jax.sharding import PartitionSpec as P

MODES = 6
LANES = 128
PARTS = 4
BF = jnp.bfloat16
F32 = jnp.float32
I32 = jnp.int32


def around(x, by):
    length = lax.axis_size("cols")
    return lax.ppermute(x, "cols", [(i, (i + by) % length) for i in range(length)])


def swap_chip(x):
    length = lax.axis_size("rows")
    return lax.ppermute(x, "rows", [(i, i ^ 1) for i in range(length)])


def swap_cross(x, turn=1):
    rows = lax.axis_size("rows")
    cols = lax.axis_size("cols")
    pairs = []
    for c in range(cols):
        for r in range(1, rows - 1, 2):
            pairs += [(r * cols + c, (r + 1) * cols + c), ((r + 1) * cols + c, r * cols + c)]
        for r in (0, rows - 1):
            pairs.append((r * cols + c, r * cols + (c ^ turn)))
    return lax.ppermute(x, ("rows", "cols"), pairs)


def dot(a, b, trans_b=False):
    return lax.dot_general(
        a, b, (((1,), (1 if trans_b else 0,)), ((), ())), preferred_element_type=F32
    )


def pack_kernel(q_ref, out_ref):
    blocks, rows, dofs = q_ref.shape
    half = blocks // 2
    groups = rows // MODES
    many = 4
    r = lax.broadcasted_iota(I32, (many * rows, many * rows), 0)
    c = lax.broadcasted_iota(I32, (many * rows, many * rows), 1)
    rl = r % rows
    perm = (r - rl) + (rl % groups) * MODES + rl // groups == c
    perm = jnp.where(perm, 1.0, 0.0).astype(BF)
    step = many * rows
    for n in range(half // many):
        a = dot(perm, q_ref[n * many : (n + 1) * many].reshape(step, dofs))
        b = dot(perm, q_ref[half + n * many : half + (n + 1) * many].reshape(step, dofs))
        lo = n * step
        out_ref[lo : lo + step, :] = a[:, :LANES].astype(BF)
        hi = half * rows + lo
        out_ref[hi : hi + step, :] = b[:, :LANES].astype(BF)
        mixed = jnp.concatenate([a[:, LANES:], b[:, LANES:]], axis=1)
        tail = blocks * rows + lo
        out_ref[tail : tail + step, :] = mixed.astype(BF)


def table_kernel(nbr_ref, aggs_ref, s_hbm, s_out, aggr_ref, aggl_ref, rel, ssem):
    slots, blocks = nbr_ref.shape
    copies = [pltpu.make_async_copy(s_hbm.at[i], s_out.at[i], ssem.at[i]) for i in range(blocks)]
    for cp in copies:
        cp.start()
    nagg, total = aggs_ref.shape
    groups = nagg // PARTS
    row = lax.axis_index("rows")
    col = lax.axis_index("cols")
    rel[...] = (aggs_ref[...] - (row - 2) * blocks).astype(F32)
    turned = []
    for d in range(PARTS):
        q = col + d
        q = jnp.where(q >= PARTS, q - PARTS, q)
        turned.append(rel[pl.ds(pl.multiple_of(q * groups, groups), groups), :])
    turned = jnp.concatenate(turned, axis=0).astype(BF)
    wanted = nbr_ref[...].T
    lane = lax.broadcasted_iota(I32, (blocks, total), 1)
    pieces = []
    for k in range(slots):
        hot = jnp.where(lane == wanted[:, k : k + 1], 1.0, 0.0).astype(BF)
        pieces.append(dot(hot, turned, True))
    aggr_ref[...] = jnp.concatenate(pieces, axis=1).astype(I32)
    sub = lax.broadcasted_iota(I32, (blocks, total), 0) + row * blocks
    own = dot(jnp.where(lane == sub, 1.0, 0.0).astype(BF), turned, True)
    src = lax.broadcasted_iota(I32, (nagg, MODES * nagg), 0)
    dst = lax.broadcasted_iota(I32, (nagg, MODES * nagg), 1)
    rows = MODES * groups
    spread = src == (dst // rows) * groups + dst % groups
    own = dot(own.astype(BF), jnp.where(spread, 1.0, 0.0).astype(BF)).astype(I32) - blocks
    mode = (lax.broadcasted_iota(I32, own.shape, 1) % rows) // groups
    aggl_ref[...] = (own // blocks) * LANES + (own % blocks) * MODES + mode
    for cp in copies:
        cp.wait()


def left_kernel(aggl_ref, w0, w1, w2, w3, lo_ref, hi_ref):
    blocks = aggl_ref.shape[0]
    half = blocks // 2
    rows = aggl_ref.shape[1] // PARTS
    first_half = lax.broadcasted_iota(I32, (3 * LANES, LANES), 1) < LANES // 2

    def placed(i):
        hot = lax.broadcasted_iota(I32, (3 * LANES, PARTS * rows), 0) == aggl_ref[i : i + 1, :]
        hot = jnp.where(hot, 1.0, 0.0).astype(BF)
        first = jnp.concatenate([w[i * rows : (i + 1) * rows] for w in (w0, w1, w2, w3)], axis=0)
        at = (blocks + i % half) * rows
        second = jnp.concatenate([w[at : at + rows] for w in (w0, w1, w2, w3)], axis=0)
        left = dot(hot, jnp.concatenate([first, second], axis=1))
        lo_ref[:, i * LANES : (i + 1) * LANES] = left[:, :LANES].astype(BF)
        return left[:, LANES:]

    for n in range(half):
        a = placed(n)
        b = placed(n + half)
        hi_ref[:, n * LANES : (n + 1) * LANES] = jnp.where(first_half, a, b).astype(BF)


def main_kernel(nbr_ref, live_ref, aggr_ref, lo_ref, hi_ref, s_ref, *rest):
    pieces = rest[: 3 * PARTS]
    chip_ref, mid_ref, cross_ref, wbuf, images, asm_lo, asm_hi, wsem = rest[3 * PARTS :]
    blocks, slots, dofs, _ = s_ref.shape
    half = blocks // 2
    quarter = pieces[0].shape[0]
    rows = quarter // (blocks + half)
    groups = rows // MODES
    reach = 5 * blocks
    chunk = slots * PARTS * groups
    row = lax.axis_index("rows")
    col = lax.axis_index("cols")
    copies = [
        pltpu.make_async_copy(p, wbuf.at[pl.ds(n * quarter, quarter)], wsem.at[n])
        for n, p in enumerate(pieces)
    ]
    for cp in copies:
        cp.start()
    low_lanes = (lax.broadcasted_iota(I32, (1, LANES), 1) < LANES // 2).astype(I32)
    odd = row % 2
    for cp in copies:
        cp.wait()

    def image(i, k):
        j = nbr_ref[k, i] - (row - 1) * blocks
        w = j // blocks
        jl = j - w * blocks
        w = jnp.where(w == 1, 0, jnp.where((w == 2) == (odd == 0), 1, 2))
        place = w * PARTS * quarter
        jh = jnp.where(jl >= half, jl - half, jl)
        first = [
            wbuf[pl.ds(pl.multiple_of(place + d * quarter + jl * rows, 16), rows), :]
            for d in range(PARTS)
        ]
        second = [
            wbuf[pl.ds(pl.multiple_of(place + d * quarter + (blocks + jh) * rows, 16), rows), :]
            for d in range(PARTS)
        ]
        keep = jnp.where((low_lanes == 1) == (jl < half), 1.0, 0.0).astype(BF)
        pj = jnp.concatenate(
            [jnp.concatenate(first, axis=0), jnp.concatenate(second, axis=0) * keep], axis=1
        )
        s = s_ref[i, k]
        tail = s[:, LANES:]
        return dot(pj, jnp.concatenate([s[:, :LANES], tail, tail], axis=1), True)

    for i in range(blocks):
        parts = [image(i, k) for k in range(slots)]
        for m in range(MODES):
            images[i, m * chunk : (m + 1) * chunk] = jnp.concatenate(
                [
                    img[d * rows + m * groups : d * rows + (m + 1) * groups]
                    for img in parts
                    for d in range(PARTS)
                ],
                axis=0,
            ).astype(BF)

    lane = lax.broadcasted_iota(I32, (1, chunk), 1) // (PARTS * groups)

    def assemble(i):
        target = jnp.where(lane + col * slots < live_ref[i], aggr_ref[i : i + 1, :], -1)
        place_t = lax.broadcasted_iota(I32, (reach, chunk), 0) == target
        place_t = jnp.where(place_t, 1.0, 0.0).astype(BF)
        tails = []
        for m in range(MODES):
            asm = dot(place_t, images[i, m * chunk : (m + 1) * chunk])
            asm_lo[m * reach : (m + 1) * reach, i * LANES : (i + 1) * LANES] = asm[
                :, :LANES
            ].astype(BF)
            tails.append(asm[:, LANES:].astype(BF))
        return tails

    for n in range(half):
        a = assemble(n)
        b = assemble(n + half)
        for m in range(MODES):
            asm_hi[m * reach : (m + 1) * reach, n * LANES : (n + 1) * LANES] = jnp.concatenate(
                [a[m], b[m]], axis=1
            )
    acc = dot(asm_lo[...], lo_ref[...], True) + dot(asm_hi[...], hi_ref[...], True)
    width = mid_ref.shape[1]
    even = odd == 0
    low = acc[:, :width]
    up = acc[:, 2 * LANES : 2 * LANES + width]
    chip_ref[...] = jnp.where(even, up, low)
    mid_ref[...] = acc[:, LANES : LANES + width]
    cross_ref[...] = jnp.where(even, low, up).astype(BF)


def share_kernel(mid_ref, chip_ref, cross_ref, o0, o1, o2, o3, tot):
    reach = mid_ref.shape[0] // MODES
    band = 7 * reach // 5
    blocks = band // 7
    piece = o0.shape[0]
    padded = o1.shape[0]
    width = tot.shape[1]

    def zeros(n):
        return jnp.zeros((n * blocks, width), F32)

    even = lax.axis_index("rows") % 2 == 0
    for m in range(MODES):
        src = slice(m * reach, (m + 1) * reach)
        chip = chip_ref[src]
        cross = cross_ref[src].astype(F32)
        above = jnp.where(even, chip, cross)
        below = jnp.where(even, cross, chip)
        tot[m * band : (m + 1) * band] = (
            jnp.concatenate([zeros(1), mid_ref[src], zeros(1)], axis=0)
            + jnp.concatenate([zeros(2), above], axis=0)
            + jnp.concatenate([below, zeros(2)], axis=0)
        )
    tot[MODES * band :] = jnp.zeros((padded - piece, width), F32)
    for d, o in enumerate((o0, o1, o2, o3)):
        c = lax.axis_index("cols") + d
        c = jnp.where(c >= PARTS, c - PARTS, c)
        o[...] = tot[pl.ds(pl.multiple_of(c * piece, 8), o.shape[0]), :].astype(o.dtype)


def on_device(stiffness, neighbors, live_counts, prolong, prolong_aggs):
    blocks, slots, dofs, _ = stiffness.shape
    rows = prolong.shape[1]
    nagg = prolong_aggs.shape[1]
    quarter = (blocks + blocks // 2) * rows
    vmem = pl.BlockSpec(memory_space=pltpu.VMEM)
    smem = pl.BlockSpec(memory_space=pltpu.SMEM)
    any_ = pl.BlockSpec(memory_space=pl.ANY)
    hbm = pl.BlockSpec(memory_space=pltpu.HBM)
    nbr = neighbors.T

    w0 = pl.pallas_call(
        pack_kernel,
        out_shape=jax.ShapeDtypeStruct((quarter, LANES), BF),
        in_specs=[vmem],
        out_specs=vmem,
        compiler_params=pltpu.CompilerParams(vmem_limit_bytes=8 * 2**20),
    )(prolong)
    w2 = around(w0, 2)
    w1 = around(w0, -1)
    w3 = around(w0, 1)
    b0 = swap_cross(w0)
    aggs = prolong_aggs.T

    s_near, aggr, aggl = pl.pallas_call(
        table_kernel,
        out_shape=[
            pltpu.VMEM(stiffness.shape, BF),
            pltpu.VMEM((blocks, slots * nagg), I32),
            pltpu.VMEM((blocks, MODES * nagg), I32),
        ],
        in_specs=[vmem, vmem, hbm],
        out_specs=[vmem] * 3,
        scratch_shapes=[
            pltpu.VMEM((nagg, prolong_aggs.shape[0]), F32),
            pltpu.SemaphoreType.DMA((blocks,)),
        ],
        compiler_params=pltpu.CompilerParams(vmem_limit_bytes=50 * 2**20),
    )(nbr, aggs, stiffness)
    w2, aggl = lax.optimization_barrier((w2, aggl))

    b1 = around(b0, -1)
    b3 = around(b0, 1)
    b2 = swap_cross(w2, 3)
    q0, q1, q2, q3, b2 = lax.optimization_barrier((w0, w1, w2, w3, b2))
    a0, a1, a2, a3 = (swap_chip(q) for q in (q0, q1, q2, q3))

    left_lo, left_hi = pl.pallas_call(
        left_kernel,
        out_shape=[
            pltpu.VMEM((3 * LANES, blocks * LANES), BF),
            pltpu.VMEM((3 * LANES, blocks * LANES // 2), BF),
        ],
        in_specs=[vmem] * 5,
        out_specs=[vmem] * 2,
        compiler_params=pltpu.CompilerParams(vmem_limit_bytes=16 * 2**20),
    )(aggl, w0, w1, w2, w3)

    reach = 5 * blocks
    out = jax.ShapeDtypeStruct((MODES * reach, blocks * MODES), F32)
    to_chip, mid, to_cross = pl.pallas_call(
        main_kernel,
        out_shape=[out, out, jax.ShapeDtypeStruct(out.shape, BF)],
        in_specs=[smem, smem, vmem, vmem, vmem, vmem] + [any_] * 12,
        out_specs=[vmem] * 3,
        scratch_shapes=[
            pltpu.VMEM((3 * PARTS * quarter, LANES), BF),
            pltpu.VMEM((blocks, slots * MODES * nagg, dofs), BF),
            pltpu.VMEM((MODES * reach, blocks * LANES), BF),
            pltpu.VMEM((MODES * reach, blocks * LANES // 2), BF),
            pltpu.SemaphoreType.DMA((3 * PARTS,)),
        ],
        compiler_params=pltpu.CompilerParams(vmem_limit_bytes=24 * 2**20),
    )(nbr, live_counts, aggr, left_lo, left_hi, s_near, w0, w1, w2, w3, a0, a1, a2, a3, b0, b1, b2, b3)
    from_cross = swap_cross(to_cross)
    from_chip = swap_chip(to_chip)
    piece = MODES * 7 * blocks // PARTS
    padded = -(-piece // 16) * 16
    sh = jax.ShapeDtypeStruct((padded, blocks * MODES), BF)
    s0, s1, s2, s3 = pl.pallas_call(
        share_kernel,
        out_shape=[jax.ShapeDtypeStruct((piece, blocks * MODES), F32), sh, sh, sh],
        in_specs=[vmem] * 3,
        out_specs=[vmem] * 4,
        scratch_shapes=[pltpu.VMEM((PARTS * piece + padded - piece, blocks * MODES), F32)],
        compiler_params=pltpu.CompilerParams(vmem_limit_bytes=8 * 2**20),
    )(mid, from_chip, from_cross)
    t1 = around(s1, 1)
    t3 = around(s3, -1)
    t2 = around(s2, 2)
    t1, t2, t3 = (t[:piece].astype(F32) for t in (t1, t2, t3))
    return ((s0 + t1) + (t2 + t3)).T


def solution(mesh):
    in_specs = (
        P("rows", "cols", None, None),
        P("rows", "cols"),
        P("rows"),
        P("rows", "cols", None),
        P(),
    )
    out_specs = P("rows", "cols")
    return jax.shard_map(
        on_device, mesh=mesh, in_specs=in_specs, out_specs=out_specs, check_vma=False
    )
```
